256 devices in a mesh: node: 16 (over y, x_hi, core), local: 16 (over z, x_lo).
Axes of the slice: x: 4 (x_hi: 2, x_lo: 2; x = x_hi * 2 + x_lo), y: 4, z: 8, core: 2. Of those that a mesh axis runs over, the one named last changes fastest.
Arguments:
- tokens: bfloat16 [32768, 3584], P(('node', 'local')), may hold values from -24 to 24
- gain_master: float32 [3584], P(('node', 'local')), may hold values from -0.5 to 0.5
- weight_master: float32 [3584, 1024], P(('node', 'local')), may hold values from -0.09375 to 0.09375
- cotangent: bfloat16 [32768, 1024], P(('node', 'local')), may hold values from -6 to 6
- w_first: float32 [3584, 1024], P(('node', 'local')), may hold values from -0.01953125 to 0.01953125
- w_second: float32 [3584, 1024], P(('node', 'local')), may hold values from 4.7683716e-07 to 7.6293945e-06
- gain_first: float32 [3584], P(('node', 'local')), may hold values from -0.009765625 to 0.009765625
- gain_second: float32 [3584], P(('node', 'local')), may hold values from 1.1920929e-07 to 1.9073486e-06
Outputs:
- keys: bfloat16 [32768, 1024], P(('node', 'local'))
- grad_tokens: bfloat16 [32768, 3584], P(('node', 'local'))
- weight_step: float32 [3584, 1024], P(('node', 'local'))
- gain_step: float32 [3584], P(('node', 'local'))
The draws below stay inside these ranges and needn't reach their ends.
All inputs are finite; a program needn't handle non-finite values.
Results may differ from the reference program's by a relative error of at most 0.015.
Values may be sent and summed in bfloat16 or wider, within the bound.
No kernel may reach another device: no remote copies, remote signals or barrier semaphores. Data moves between devices by JAX's collectives and lax.ppermute only.
A program may use at most 128 MiB of HBM per device.

```python
import math
import jax
import jax.numpy as jnp
from jax import lax

D = 3584
BLOCK = 128
TOK_DEV = 128
KV = 1024
TOKENS = 32768
N_NODE = 16
N_LOCAL = 16


def raised(entries, own_key, source, target, shards_of, factor):
    def block_of(axis_at):
        return (jnp.arange(entries.shape[axis_at]) // (entries.shape[axis_at] // shards_of)).reshape((-1,) + (1,) * (entries.ndim - 1 - axis_at))

    one_side = jax.random.permutation(own_key, shards_of)[block_of(target)]
    other_side = (block_of(target) + shards_of // 2) % shards_of
    return jnp.where((block_of(source) == one_side) | (block_of(source) == other_side), factor * entries, entries)


def block_levels(stream_key, extent, cuts, smallest, largest):
    def one(axis_at, blocks):
        heights = jax.random.uniform(jax.random.fold_in(jax.random.fold_in(stream_key, 6), axis_at), (blocks,), jnp.float32, smallest / len(cuts), largest / len(cuts))
        return jnp.repeat(jnp.exp(heights), extent[axis_at] // blocks).reshape((-1,) + (1,) * (len(extent) - axis_at - 1))

    level = one(*cuts[0])
    for cut in cuts[1:]:
        level = level * one(*cut)
    return level


def gaussian(rng, shape, spread, most, cuts=(), held_as=jnp.bfloat16):
    result = spread * jax.random.normal(rng, shape, jnp.float32)
    if cuts:
        result = result * block_levels(rng, shape, cuts, -0.22, 0.18)
    return jnp.clip(result, -most, most).astype(held_as)


def gaussian_with(own_key, dims, deviation, reach, pieces, heavy, dtype=jnp.bfloat16):
    values = deviation * jax.random.normal(own_key, dims, jnp.float32)
    if pieces:
        values = values * block_levels(own_key, dims, pieces, -0.22, 0.18)
    return jnp.clip(raised(values, jax.random.fold_in(own_key, 3), *heavy), -reach, reach).astype(dtype)


def setup_inputs(seed: int = 0) -> dict:
    seeds = jax.random.split(jax.random.key(seed), 9)
    tokens = gaussian_with(seeds[0], (TOKENS, D), 1.0, 24.0, ((0, 256),), (0, 1, 256, 6.0))
    gain_master = jnp.clip(jax.random.uniform(seeds[1], (D,), jnp.float32, -0.5, 0.5) * block_levels(seeds[1], (D,), ((0, 256),), -0.4, 0.0), -0.5, 0.5)
    weight_master = gaussian(seeds[2], (D, KV), D ** -0.5, 0.09375, ((0, 256),), jnp.float32)
    cotangent = gaussian(seeds[3], (TOKENS, KV), 1.0, 6.0, ((0, 256),))
    w_first = gaussian(seeds[4], (D, KV), (0.25 * TOKENS ** -0.5), 0.01953125, ((0, 256),), jnp.float32)
    w_second = jnp.clip(jnp.exp(math.log(7.62939453125e-06) - 2.7725887 * jax.random.uniform(seeds[5], (D, KV), jnp.float32) ** block_levels(seeds[5], (D, KV), ((0, 256),), -0.2, 0.2)), 4.76837158203125e-07, 7.62939453125e-06)
    gain_first = gaussian(seeds[6], (D,), (0.125 * TOKENS ** -0.5), 0.009765625, ((0, 256),), jnp.float32)
    gain_second = jnp.clip(jnp.exp(math.log(1.9073486328125e-06) - 2.7725887 * jax.random.uniform(seeds[7], (D,), jnp.float32) ** block_levels(seeds[7], (D,), ((0, 256),), -0.2, 0.2)), 1.1920928955078125e-07, 1.9073486328125e-06)
    return {"tokens": tokens, "gain_master": gain_master, "weight_master": weight_master, "cotangent": cotangent, "w_first": w_first, "w_second": w_second, "gain_first": gain_first, "gain_second": gain_second}


eps_norm = 1e-06
beta_one = 0.9
beta_two = 0.999
eps_adam = 1e-08

def quantize(master):
    shard_rows, out_width = master.shape
    runs = master.reshape(shard_rows, out_width // BLOCK, BLOCK)
    scales = (lax.optimization_barrier(jnp.max(jnp.abs(runs), axis=2)) + 1e-06) / 127.0
    levels = jnp.floor(runs / scales[:, :, None] + 0.5)
    return (levels.reshape(shard_rows, out_width), scales)

def adam_step(grad, first, second):
    first = beta_one * first + (1.0 - beta_one) * grad
    second = beta_two * second + (1.0 - beta_two) * grad * grad
    return first / (jnp.sqrt(second) + eps_adam)

def reference(tokens, gain_master, weight_master, cotangent, w_first, w_second, gain_first, gain_second):
    levels, scales = quantize(weight_master)
    weight = (levels.reshape(D, KV // BLOCK, BLOCK) * scales[:, :, None]).reshape(D, KV).astype(jnp.bfloat16)
    one_gain = 1.0 + gain_master
    blocks_x = tokens.reshape(N_NODE * N_LOCAL, TOK_DEV, D)
    blocks_g = cotangent.reshape(N_NODE * N_LOCAL, TOK_DEV, KV)

    def step(carry, pair):
        weight_sum, gain_sum = carry
        block_x, block_g = pair
        values = block_x.astype(jnp.float32)
        inv_rms = lax.rsqrt(lax.optimization_barrier(jnp.mean(values * values, axis=1, keepdims=True)) + eps_norm)
        normed = values * inv_rms
        hidden = (normed * one_gain).astype(jnp.bfloat16)
        keys = jnp.dot(hidden, weight, preferred_element_type=jnp.float32).astype(jnp.bfloat16)
        grad_hidden = jnp.dot(block_g, weight.T, preferred_element_type=jnp.float32)
        scaled = grad_hidden * one_gain
        inner = lax.optimization_barrier(jnp.mean(scaled * normed, axis=1, keepdims=True))
        grad_x = (inv_rms * (scaled - normed * inner)).astype(jnp.bfloat16)
        weight_sum = weight_sum + jnp.dot(hidden.T, block_g, preferred_element_type=jnp.float32)
        gain_sum = gain_sum + lax.optimization_barrier(jnp.sum(grad_hidden * normed, axis=0))
        return ((weight_sum, gain_sum), (keys, grad_x))
    start = (jnp.zeros((D, KV), jnp.float32), jnp.zeros((D,), jnp.float32))
    (weight_sum, gain_sum), (keys, grad_x) = lax.scan(step, start, (blocks_x, blocks_g))
    weight_grad = weight_sum / TOKENS
    gain_grad = gain_sum / TOKENS
    weight_step = adam_step(weight_grad, w_first, w_second)
    gain_step = adam_step(gain_grad, gain_first, gain_second)
    return (keys.reshape(TOKENS, KV), grad_x.reshape(TOKENS, D), weight_step, gain_step)
```

```python
import jax
import jax.numpy as jnp
from jax import lax
from jax.sharding import Mesh, PartitionSpec as P

RUN = 128
AXES = ("y", "xh", "core", "z", "xl")
SIZES = (4, 2, 2, 8, 2)

eps_norm = 1e-06
beta_one = 0.9
beta_two = 0.999
eps_adam = 1e-08

bf16 = jnp.bfloat16
f32 = jnp.float32


def index_of(y, x, z, c):
    return (((y * 2 + x // 2) * 2 + c) * 8 + z) * 2 + x % 2


def move(value, target):
    pairs = []
    for y in range(4):
        for x in range(4):
            for z in range(8):
                for c in range(2):
                    ty, tx, tz, tc = target(y, x, z, c)
                    pairs.append((index_of(y, x, z, c), index_of(ty % 4, tx % 4, tz % 8, tc % 2)))
    return lax.ppermute(value, AXES, pairs)


def along_y(value, step):
    return move(value, lambda y, x, z, c: (y + step, x, z, c))


def along_z(value, step):
    return move(value, lambda y, x, z, c: (y, x, z + step, c))


def across_x(value):
    return move(value, lambda y, x, z, c: (y, x + 2, z, c))


def beside_x(value):
    return move(value, lambda y, x, z, c: (y, x ^ 1, z, c))


def swap(value):
    return move(value, lambda y, x, z, c: (y, x, z, 1 - c))


def pick(value, index):
    return lax.dynamic_index_in_dim(value, index, 0, keepdims=False)


def dot(a, b, ca, cb):
    return lax.dot_general(a, b, (((ca,), (cb,)), ((), ())), preferred_element_type=f32)


def ordered(first, own, other):
    return jnp.stack([jnp.where(first, own, other), jnp.where(first, other, own)])


def rolled(blocks, start):
    return lax.dynamic_slice_in_dim(jnp.concatenate([blocks, blocks]), start, blocks.shape[0], 0)


def quantized(master):
    rows, width = master.shape
    runs = master.reshape(rows, width // RUN, RUN)
    scales = (jnp.max(jnp.abs(runs), axis=2) + 1e-06) / 127.0
    levels = jnp.floor(runs / scales[:, :, None] + 0.5)
    return (levels * scales[:, :, None]).reshape(rows, width)


def adam_step(grad, first, second):
    first = beta_one * first + (1.0 - beta_one) * grad
    second = beta_two * second + (1.0 - beta_two) * grad * grad
    return first / (jnp.sqrt(second) + eps_adam)


def gather_weight(shard, z, xh, xl):
    rows, width = shard.shape
    two = ordered(xl == 0, shard, beside_x(shard)).reshape(2 * rows, width)
    near = jnp.stack([along_z(two, 1), two, along_z(two, -1)])
    below, above = along_z(near, 3), along_z(near[:2], -3)
    cycle = jnp.concatenate([below, near, above])
    own = rolled(cycle, (4 - z) % 8).reshape(16 * rows, width)
    return ordered(xh == 0, own, across_x(own)).reshape(32 * rows, width)


def scatter_sum(term, z, xh, xl):
    rows, width = term.shape
    halves = term.reshape(2, rows // 2, width)
    part = pick(halves, xh) + across_x(pick(halves, 1 - xh).astype(bf16)).astype(f32)
    blocks = rolled(part.reshape(8, rows // 16, width), (z + 4) % 8)
    sent = blocks.astype(bf16)
    low = along_z(jnp.concatenate([sent[6:], sent[:1]]), 3).astype(f32)
    high = along_z(sent[1:3], -3).astype(f32)
    to_next = (blocks[5] + low[2] + high[1]).astype(bf16)
    to_last = (blocks[3] + low[0]).astype(bf16)
    mine = blocks[4] + low[1] + high[0]
    mine = mine + along_z(to_next, 1).astype(f32) + along_z(to_last, -1).astype(f32)
    pair = mine.reshape(2, rows // 32, width)
    return pick(pair, xl) + beside_x(pick(pair, 1 - xl).astype(bf16)).astype(f32)


def body(tokens, gain_master, weight_master, cotangent, w_first, w_second, gain_first, gain_second):
    y, xh, c, z, xl = [lax.axis_index(name) for name in AXES]
    tok_count, model_width = tokens.shape
    key_width = cotangent.shape[1]
    total = tok_count * 256
    block = model_width // 16

    weight = quantized(weight_master)
    one_gain = 1.0 + gain_master
    shard = (weight * one_gain[:, None]).astype(bf16)
    gathered = gather_weight(shard, z, xh, xl)

    steps = (1, -1, 2)
    cot_own = [cotangent] + [along_y(cotangent, s) for s in steps]
    cot_other = [swap(v) for v in cot_own]
    cots = jnp.concatenate([v for pair in zip(cot_own, cot_other) for v in pair])

    values = tokens.astype(f32)
    inv_rms = lax.rsqrt(jnp.mean(values * values, axis=1, keepdims=True) + eps_norm)
    normed = values * inv_rms
    flipped = normed.astype(bf16).T.reshape(4, 2, 2, block, tok_count).transpose(2, 0, 1, 3, 4)
    flipped = flipped.reshape(2, 4, 2 * block, tok_count)
    pieces = jnp.concatenate([pick(flipped, c), swap(pick(flipped, 1 - c))], axis=2)
    features = jnp.concatenate(
        [pick(pieces, y)] + [along_y(pick(pieces, (y + s) % 4), s) for s in steps], axis=1
    )

    term = dot(features, cots, 1, 0)
    summed = scatter_sum(term, z, xh, xl)

    part_keys = dot(features, gathered, 0, 0).reshape(4, 2, tok_count, key_width)
    part_keys = part_keys[:, 0] + swap(part_keys[:, 1].astype(bf16)).astype(f32)
    part_scaled = dot(gathered, cots, 1, 1).astype(bf16).reshape(2 * block, 4, 2 * tok_count)
    keys = part_keys[0]
    home = [part_scaled[:, 0]]
    for j, s in enumerate(steps):
        keys = keys + along_y(part_keys[j + 1].astype(bf16), -s).astype(f32)
        home.append(along_y(part_scaled[:, j + 1], -s))
    home = jnp.stack([home[2], home[0], home[1], home[3]])
    home = rolled(home, (1 - y) % 4)
    scaled = ordered(c == 0, home[:, :, :tok_count], swap(home[:, :, tok_count:]))
    scaled = scaled.reshape(2, 4, 2, block, tok_count).transpose(1, 2, 0, 3, 4)
    scaled = scaled.reshape(model_width, tok_count).T.astype(f32)

    inner = jnp.mean(scaled * normed, axis=1, keepdims=True)
    grad_tokens = (inv_rms * (scaled - normed * inner)).astype(bf16)

    weight_grad = summed * one_gain[:, None] / total
    gain_grad = jnp.sum(weight * summed, axis=1) / total
    weight_step = adam_step(weight_grad, w_first, w_second)
    gain_step = adam_step(gain_grad, gain_first, gain_second)
    return (keys.astype(bf16), grad_tokens, weight_step, gain_step)


def solution(mesh):
    fine = Mesh(mesh.devices.reshape(SIZES), AXES)
    matrix, vector = P(AXES, None), P(AXES)
    return jax.shard_map(
        body,
        mesh=fine,
        in_specs=(matrix, vector, matrix, matrix, matrix, matrix, vector, vector),
        out_specs=(matrix, matrix, matrix, vector),
        check_vma=False,
    )
```

```python
import jax
import jax.numpy as jnp
import numpy as np
from jax import lax
from jax.experimental import pallas as pl
from jax.experimental.pallas import tpu as pltpu
from jax.sharding import Mesh, PartitionSpec as P

RUN = 128
AXES = ("y", "xh", "core", "z", "xl")
SIZES = (4, 2, 2, 8, 2)

eps_norm = 1e-06
beta_one = 0.9
beta_two = 0.999
eps_adam = 1e-08

bf16 = jnp.bfloat16
f32 = jnp.float32


def index_of(y, x, z, c):
    return (((y * 2 + x // 2) * 2 + c) * 8 + z) * 2 + x % 2


def move(value, target):
    pairs = []
    for y in range(4):
        for x in range(4):
            for z in range(8):
                for c in range(2):
                    ty, tx, tz, tc = target(y, x, z, c)
                    pairs.append((index_of(y, x, z, c), index_of(ty % 4, tx % 4, tz % 8, tc % 2)))
    return lax.ppermute(value, AXES, pairs)


def along_y(value, step):
    return move(value, lambda y, x, z, c: (y + step, x, z, c))


def along_x(value, flip):
    return move(value, lambda y, x, z, c: (y, x ^ flip, z, c))


def swap(value):
    return move(value, lambda y, x, z, c: (y, x, z, 1 - c))


STEPS = (2, 1, -1)


def dot(a, b, ca, cb):
    return lax.dot_general(a, b, (((ca,), (cb,)), ((), ())), preferred_element_type=f32)


def call(kernel, outs, scratch, flops, *operands):
    specs = [pl.BlockSpec(memory_space=pltpu.SMEM if v.dtype == jnp.int32 and v.ndim == 1 else pltpu.VMEM) for v in operands]
    moved = sum(v.size * v.dtype.itemsize for v in operands)
    return pl.pallas_call(
        kernel,
        out_shape=[jax.ShapeDtypeStruct(shape, dtype) for shape, dtype in outs],
        in_specs=specs,
        out_specs=[pl.BlockSpec(memory_space=pltpu.VMEM)] * len(outs),
        scratch_shapes=[pltpu.VMEM(shape, dtype) for shape, dtype in scratch],
        compiler_params=pltpu.CompilerParams(vmem_limit_bytes=24 * 2**20),
        cost_estimate=pl.CostEstimate(flops=flops, bytes_accessed=moved, transcendentals=0),
    )(*operands)


def exchange_z(blocks):
    return lax.all_to_all(blocks, "z", split_axis=0, concat_axis=0, tiled=True)


def adam_step(grad, first, second):
    first = beta_one * first + (1.0 - beta_one) * grad
    second = beta_two * second + (1.0 - beta_two) * grad * grad
    return first / (jnp.sqrt(second) + eps_adam)


def feature_table(quarter, rows):
    place = np.arange(quarter)
    r, z, k, other = place % rows, place // rows % 8, place // (8 * rows) % 4, place // (32 * rows)
    table = []
    for x in range(4):
        for c in range(2):
            at = x ^ k
            table.append((((at // 2) * 2 + (c ^ other)) * 8 + z) * 2 * rows + at % 2 * rows + r)
    return np.stack(table).astype(np.int32)


def one_hot(where, table):
    width = table.shape[1]
    place = table[pl.ds(where[1], 1), :]
    feature = lax.broadcasted_iota(jnp.int32, (width, width), 0)
    return jnp.where(feature == place, 1.0, 0.0).astype(bf16)


def quantize_kernel(master, gain, shard):
    columns = []
    for n in range(master.shape[1] // RUN):
        run = master[:, n * RUN : (n + 1) * RUN]
        scale = (jnp.max(jnp.abs(run), axis=1, keepdims=True) + 1e-06) / 127.0
        columns.append(jnp.floor(run / scale + 0.5) * scale)
    value = (jnp.concatenate(columns, axis=1) * (1.0 + gain[...])).astype(bf16)
    for n in range(shard.shape[0]):
        shard[n] = value


def norm_kernel(where, table, tokens, own, two, up, down, inv_rms, rounded):
    values = tokens[...].astype(f32)
    inv = lax.rsqrt(jnp.mean(values * values, axis=1, keepdims=True) + eps_norm)
    inv_rms[...] = inv
    rounded[...] = (values * inv).astype(bf16)
    choice = one_hot(where, table)
    width = choice.shape[0]
    for s, out in zip(STEPS + (0,), (two, up, down, own)):
        at = pl.multiple_of(lax.rem(where[0] + s + 4, 4) * width, 128)
        part = rounded[:, pl.ds(at, width)]
        out[...] = jnp.dot(part, choice, preferred_element_type=f32).astype(bf16)


def term_kernel(*refs):
    feats, cots, outs, theirs, fs, cs = refs[:4], refs[4:8], refs[8:12], refs[12], refs[13], refs[14]
    tok = feats[0].shape[0]
    for j in range(4):
        fs[j * tok : (j + 1) * tok] = feats[j][...]
        cs[j * tok : (j + 1) * tok] = cots[j][...]
    chunk = outs[0].shape[0]
    for k in range(4):
        outs[k][...] = dot(fs[:, k * chunk : (k + 1) * chunk], cs[...], 0, 0)
    theirs[...] = dot(fs[:, 4 * chunk :], cs[...], 0, 0).astype(bf16)


def home_kernel(*refs):
    chunks, feats, cots, outs = refs[:8], refs[8:12], refs[12:16], refs[16:20]
    ws, fs, cs = refs[20:]
    tok, rows = feats[0].shape[0], chunks[0].shape[0]
    for n in range(8):
        ws[n * rows : (n + 1) * rows] = chunks[n][...]
    for j in range(4):
        fs[j * tok : (j + 1) * tok] = feats[j][...]
        cs[j * tok : (j + 1) * tok] = cots[j][...]
    scaled = dot(cs[...], ws[...], 1, 1).astype(bf16)
    for j in range(4):
        outs[j][:, : 8 * rows] = scaled[j * tok : (j + 1) * tok]
    keys = dot(fs[...], ws[...], 1, 0).astype(bf16)
    for j in range(4):
        outs[j][:, 8 * rows :] = keys[j * tok : (j + 1) * tok]


def last_kernel(where, table, tokens, inv_rms, own, two, up, down, keys, grad, scaled):
    choice = one_hot(where, table)
    width = choice.shape[0]
    total = jnp.zeros(keys.shape, f32)
    for s, ref in zip((0,) + STEPS, (own, two, up, down)):
        total = total + ref[:, width:].astype(f32)
        at = pl.multiple_of(lax.rem(where[0] + s + 4, 4) * width, 128)
        scaled[:, pl.ds(at, width)] = dot(ref[:, :width], choice, 1, 1)
    keys[...] = total.astype(bf16)
    inv = inv_rms[...]
    normed = tokens[...].astype(f32) * inv
    inner = jnp.mean(scaled[...] * normed, axis=1, keepdims=True)
    grad[...] = (inv * (scaled[...] - normed * inner)).astype(bf16)


def body(tokens, gain_master, weight_master, cotangent, w_first, w_second, gain_first, gain_second):
    y, xh, c, z, xl = [lax.axis_index(name) for name in AXES]
    tok_count, model_width = tokens.shape
    shard_rows, key_width = weight_master.shape
    total = tok_count * 256
    quarter = model_width // 4
    eighth = quarter // 2
    chunk = eighth // 4
    macs = tok_count * quarter * 4
    where = jnp.stack([y, 4 * xh + 2 * xl + c]).astype(jnp.int32)
    table = jnp.asarray(feature_table(quarter, shard_rows))

    one_gain = 1.0 + gain_master
    (shard,) = call(quantize_kernel, [((8, shard_rows, key_width), bf16)], [], 100000, weight_master, gain_master[:, None])
    column = exchange_z(shard).reshape(chunk, key_width)

    own, *sends, inv_rms = call(
        norm_kernel,
        [((tok_count, quarter), bf16)] * 4 + [((tok_count, 1), f32)],
        [((tok_count, model_width), bf16)],
        2 * macs * quarter,
        where, table, tokens,
    )
    column, sends = lax.optimization_barrier((column, sends))
    feats = [own] + [along_y(v, s) for v, s in zip(sends, STEPS)]
    cots = [cotangent] + [along_y(cotangent, s) for s in STEPS]
    mine = [column] + [along_x(column, k) for k in (1, 2, 3)]
    gathered = mine + [swap(v) for v in mine]

    *term, theirs = call(
        term_kernel,
        [((chunk, key_width), f32)] * 4 + [((eighth, key_width), bf16)],
        [((4 * tok_count, quarter), bf16), ((4 * tok_count, key_width), bf16)],
        2 * macs * key_width,
        *feats, *cots,
    )
    theirs = swap(theirs).astype(f32)
    term = [v + theirs[k * chunk : (k + 1) * chunk] for k, v in enumerate(term)]
    summed = term[0]
    for k in (1, 2, 3):
        summed = summed + along_x(term[k].astype(bf16), k).astype(f32)
    summed = exchange_z(summed.astype(bf16).reshape(8, shard_rows, key_width))
    summed = jnp.sum(summed.astype(f32), axis=0)

    parts = call(
        home_kernel,
        [((tok_count, quarter + key_width), bf16)] * 4,
        [((quarter, key_width), bf16), ((4 * tok_count, quarter), bf16), ((4 * tok_count, key_width), bf16)],
        4 * macs * key_width,
        *gathered, *feats, *cots,
    )
    home = [parts[0]] + [along_y(v, -s) for v, s in zip(parts[1:], STEPS)]
    keys, grad_tokens = call(
        last_kernel,
        [((tok_count, key_width), bf16), ((tok_count, model_width), bf16)],
        [((tok_count, model_width), f32)],
        2 * macs * quarter,
        where, table, tokens, inv_rms, *home,
    )

    runs = weight_master.reshape(shard_rows, key_width // RUN, RUN)
    scales = (jnp.max(jnp.abs(runs), axis=2, keepdims=True) + 1e-06) / 127.0
    weight = (jnp.floor(runs / scales + 0.5) * scales).reshape(shard_rows, key_width)
    weight_grad = summed * one_gain[:, None] / total
    gain_grad = jnp.sum(weight * summed, axis=1) / total
    weight_step = adam_step(weight_grad, w_first, w_second)
    gain_step = adam_step(gain_grad, gain_first, gain_second)
    return (keys, grad_tokens, weight_step, gain_step)


def solution(mesh):
    fine = Mesh(mesh.devices.reshape(SIZES), AXES)
    matrix, vector = P(AXES, None), P(AXES)
    return jax.shard_map(
        body,
        mesh=fine,
        in_specs=(matrix, vector, matrix, matrix, matrix, matrix, vector, vector),
        out_specs=(matrix, matrix, matrix, vector),
        check_vma=False,
    )
```

```python
import functools

import jax
import jax.numpy as jnp
import numpy as np
from jax import lax
from jax.experimental import pallas as pl
from jax.experimental.pallas import tpu as pltpu
from jax.sharding import Mesh, PartitionSpec as P

RUN = 128
AXES = ("y", "xh", "core", "z", "xl")
SIZES = (4, 2, 2, 8, 2)

eps_norm = 1e-06
beta_one = 0.9
beta_two = 0.999
eps_adam = 1e-08

bf16 = jnp.bfloat16
f32 = jnp.float32


def index_of(y, x, z, c):
    return (((y * 2 + x // 2) * 2 + c) * 8 + z) * 2 + x % 2


def move(value, target):
    pairs = []
    for y in range(4):
        for x in range(4):
            for z in range(8):
                for c in range(2):
                    ty, tx, tz, tc = target(y, x, z, c)
                    pairs.append((index_of(y, x, z, c), index_of(ty % 4, tx % 4, tz % 8, tc % 2)))
    return lax.ppermute(value, AXES, pairs)


def along_y(value, step):
    return move(value, lambda y, x, z, c: (y + step, x, z, c))


def along_x(value, flip):
    return move(value, lambda y, x, z, c: (y, x ^ flip, z, c))


def swap(value):
    return move(value, lambda y, x, z, c: (y, x, z, 1 - c))


STEPS = (2, 1, -1)


def dot(a, b, ca, cb):
    return lax.dot_general(a, b, (((ca,), (cb,)), ((), ())), preferred_element_type=f32)


def call(kernel, outs, scratch, flops, *operands):
    specs = [pl.BlockSpec(memory_space=pltpu.SMEM if v.dtype == jnp.int32 and v.ndim == 1 else pltpu.VMEM) for v in operands]
    moved = sum(v.size * v.dtype.itemsize for v in operands)
    return pl.pallas_call(
        kernel,
        out_shape=[jax.ShapeDtypeStruct(shape, dtype) for shape, dtype in outs],
        in_specs=specs,
        out_specs=[pl.BlockSpec(memory_space=pltpu.VMEM)] * len(outs),
        scratch_shapes=[pltpu.VMEM(shape, dtype) for shape, dtype in scratch],
        compiler_params=pltpu.CompilerParams(vmem_limit_bytes=16 * 2**20),
        cost_estimate=pl.CostEstimate(flops=flops, bytes_accessed=moved, transcendentals=0),
    )(*operands)


def exchange_z(blocks):
    return lax.all_to_all(blocks, "z", split_axis=0, concat_axis=0, tiled=True)


def adam_step(grad, first, second):
    first = beta_one * first + (1.0 - beta_one) * grad
    second = beta_two * second + (1.0 - beta_two) * grad * grad
    return first / (jnp.sqrt(second) + eps_adam)


def feature_table(quarter, rows):
    place = np.arange(quarter)
    r, z, k, other = place % rows, place // rows % 8, place // (8 * rows) % 4, place // (32 * rows)
    table = []
    for x in range(4):
        for c in range(2):
            at = x ^ k
            table.append((((at // 2) * 2 + (c ^ other)) * 8 + z) * 2 * rows + at % 2 * rows + r)
    return np.stack(table).astype(np.int32)


def one_hot(where, table):
    width = table.shape[1]
    place = table[pl.ds(where[1], 1), :]
    feature = lax.broadcasted_iota(jnp.int32, (width, width), 0)
    return jnp.where(feature == place, 1.0, 0.0).astype(bf16)


def column_of(row):
    n = row.shape[1]
    same = lax.broadcasted_iota(jnp.int32, (n, n), 0) == lax.broadcasted_iota(jnp.int32, (n, n), 1)
    return jnp.sum(jnp.where(same, jnp.broadcast_to(row, (n, n)), 0.0), axis=1, keepdims=True)


def row_of(column):
    n = column.shape[0]
    same = lax.broadcasted_iota(jnp.int32, (n, n), 0) == lax.broadcasted_iota(jnp.int32, (n, n), 1)
    return jnp.sum(jnp.where(same, jnp.broadcast_to(column, (n, n)), 0.0), axis=0, keepdims=True)


def quantize_kernel(master, gain, shard, weight):
    one_gain = 1.0 + column_of(gain[...])
    for n in range(master.shape[1] // RUN):
        at = slice(n * RUN, (n + 1) * RUN)
        run = master[:, at]
        scale = (jnp.max(jnp.abs(run), axis=1, keepdims=True) + 1e-06) / 127.0
        value = jnp.floor(run / scale + 0.5) * scale
        weight[:, at] = value
        value = (value * one_gain).astype(bf16)
        for m in range(shard.shape[0]):
            shard[m, :, at] = value


def norm_kernel(where, table, tokens, own, two, up, down, inv_rms, rounded):
    values = tokens[...].astype(f32)
    inv = lax.rsqrt(jnp.mean(values * values, axis=1, keepdims=True) + eps_norm)
    inv_rms[...] = inv
    rounded[...] = (values * inv).astype(bf16)
    choice = one_hot(where, table)
    width = choice.shape[0]
    for s, out in zip(STEPS + (0,), (two, up, down, own)):
        at = pl.multiple_of(lax.rem(where[0] + s + 4, 4) * width, 128)
        part = rounded[:, pl.ds(at, width)]
        out[...] = jnp.dot(part, choice, preferred_element_type=f32).astype(bf16)


def term_kernel(*refs):
    feats, cots, outs, theirs, fs, cs = refs[:4], refs[4:8], refs[8:12], refs[12], refs[13], refs[14]
    tok = feats[0].shape[0]
    for j in range(4):
        fs[j * tok : (j + 1) * tok] = feats[j][...]
        cs[j * tok : (j + 1) * tok] = cots[j][...]
    chunk = outs[0].shape[0]
    theirs[...] = dot(fs[:, 4 * chunk :], cs[...], 0, 0).astype(bf16)
    for k in range(4):
        outs[k][...] = dot(fs[:, k * chunk : (k + 1) * chunk], cs[...], 0, 0)


def home_kernel(*refs):
    chunks, fs, cs, outs, ws = refs[:8], refs[8], refs[9], refs[10:14], refs[14]
    rows, width = chunks[0].shape[0], ws.shape[0]
    for n in range(8):
        ws[n * rows : (n + 1) * rows] = chunks[n][...]
    tok = outs[0].shape[0]
    for j in (1, 2, 3, 0):
        at = slice(j * tok, (j + 1) * tok)
        outs[j][:, :width] = dot(cs[at], ws[...], 1, 1).astype(bf16)
        outs[j][:, width:] = dot(fs[at], ws[...], 1, 0).astype(bf16)


def chunk_kernel(mine, theirs, one, two, three, out, total):
    rows = out.shape[1]
    total[...] = mine[...] + theirs[...].astype(f32) + one[...].astype(f32) + two[...].astype(f32) + three[...].astype(f32)
    for n in range(out.shape[0]):
        out[n] = total[n * rows : (n + 1) * rows].astype(bf16)


def place(where, step, width):
    return pl.multiple_of(lax.rem(where[0] + step + 4, 4) * width, 128)


def early_kernel(where, table, tokens, own, two, scaled, inner, keys, choice):
    choice[...] = one_hot(where, table)
    width = choice.shape[0]
    total = jnp.zeros(inner.shape, f32)
    for n, (s, ref) in enumerate(zip((0, 2), (own, two))):
        part = dot(ref[:, :width], choice[...], 1, 1)
        scaled[:, n * width : (n + 1) * width] = part
        total += jnp.sum(part * tokens[:, pl.ds(place(where, s, width), width)].astype(f32), axis=1, keepdims=True)
    inner[...] = total
    keys[...] = own[:, width:].astype(f32) + two[:, width:].astype(f32)


def last_kernel(where, tokens, inv_rms, up, down, early, early_inner, early_keys, choice, keys, grad, scaled):
    width = choice.shape[0]
    inv = inv_rms[...]
    inner = early_inner[...]
    for n, (s, ref) in enumerate(zip((1, -1), (up, down))):
        part = dot(ref[:, :width], choice[...], 1, 1)
        scaled[:, n * width : (n + 1) * width] = part
        inner += jnp.sum(part * tokens[:, pl.ds(place(where, s, width), width)].astype(f32), axis=1, keepdims=True)
    keys[...] = (early_keys[...] + up[:, width:].astype(f32) + down[:, width:].astype(f32)).astype(bf16)
    inner = inner * inv * (1.0 / tokens.shape[1])
    for n, s in enumerate((0, 2, 1, -1)):
        at = pl.ds(place(where, s, width), width)
        normed = tokens[:, at].astype(f32) * inv
        ref = (early, scaled)[n // 2]
        part = ref[:, n % 2 * width : (n % 2 + 1) * width]
        grad[:, at] = (inv * (part - normed * inner)).astype(bf16)


def step_kernel(count, summed, weight, gain, w_first, w_second, g_first, g_second, w_step, g_step):
    grad = summed[0].astype(f32)
    for n in range(1, summed.shape[0]):
        grad = grad + summed[n].astype(f32)
    one_gain = 1.0 + column_of(gain[...])
    w_step[...] = adam_step(grad * one_gain / count, w_first[...], w_second[...])
    gain_grad = row_of(jnp.sum(weight[...] * grad, axis=1, keepdims=True)) / count
    g_step[...] = adam_step(gain_grad, g_first[...], g_second[...])


def body(tokens, gain_master, weight_master, cotangent, w_first, w_second, gain_first, gain_second):
    y, xh, c, z, xl = [lax.axis_index(name) for name in AXES]
    tok_count, model_width = tokens.shape
    shard_rows, key_width = weight_master.shape
    total = tok_count * 256
    quarter = model_width // 4
    eighth = quarter // 2
    chunk = eighth // 4
    macs = tok_count * quarter * 4
    where = jnp.stack([y, 4 * xh + 2 * xl + c]).astype(jnp.int32)
    table = jnp.asarray(feature_table(quarter, shard_rows))

    gain_row = gain_master[None]
    shard, weight = call(
        quantize_kernel,
        [((8, shard_rows, key_width), bf16), ((shard_rows, key_width), f32)],
        [],
        100000,
        weight_master, gain_row,
    )
    column = exchange_z(shard).reshape(chunk, key_width)

    own, *sends, inv_rms = call(
        norm_kernel,
        [((tok_count, quarter), bf16)] * 4 + [((tok_count, 1), f32)],
        [((tok_count, model_width), bf16)],
        2 * macs * quarter,
        where, table, tokens,
    )
    shard, cot_sent = lax.optimization_barrier((shard, cotangent))
    cots = [cotangent] + [along_y(cot_sent, s) for s in STEPS]
    column, cots = lax.optimization_barrier((column, cots))
    feats = [own] + [along_y(v, s) for v, s in zip(sends, STEPS)]
    mine = [column] + [along_x(column, k) for k in (1, 2, 3)]

    feats, mine = lax.optimization_barrier((feats, mine))
    gathered = mine + [swap(v) for v in mine]
    *term, theirs, all_feats, all_cots = call(
        term_kernel,
        [((chunk, key_width), f32)] * 4
        + [((eighth, key_width), bf16), ((4 * tok_count, quarter), bf16), ((4 * tok_count, key_width), bf16)],
        [],
        2 * macs * key_width,
        *feats, *cots,
    )
    theirs = swap(theirs).reshape(4, chunk, key_width)
    moved = [(term[k] + theirs[k].astype(f32)).astype(bf16) for k in (1, 2, 3)]
    moved = [along_x(v, k) for k, v in zip((1, 2, 3), moved)]
    (summed,) = call(
        chunk_kernel,
        [((8, shard_rows, key_width), bf16)],
        [((chunk, key_width), f32)],
        100000,
        term[0], theirs[0], *moved,
    )
    summed = exchange_z(summed)
    weight_step, gain_step = call(
        functools.partial(step_kernel, total),
        [((shard_rows, key_width), f32), ((1, shard_rows), f32)],
        [],
        100000,
        summed, weight, gain_row, w_first, w_second, gain_first[None], gain_second[None],
    )

    parts = call(
        home_kernel,
        [((tok_count, quarter + key_width), bf16)] * 4,
        [((quarter, key_width), bf16)],
        4 * macs * key_width,
        *gathered, all_feats, all_cots,
    )
    home = [parts[0]] + [along_y(v, -s) for v, s in zip(parts[1:], STEPS)]
    half = (tok_count, 2 * quarter)
    early = call(
        early_kernel,
        [(half, f32), ((tok_count, 1), f32), ((tok_count, key_width), f32), ((quarter, quarter), bf16)],
        [],
        macs * quarter,
        where, table, tokens, home[0], home[1],
    )
    keys, grad_tokens = call(
        last_kernel,
        [((tok_count, key_width), bf16), ((tok_count, model_width), bf16)],
        [(half, f32)],
        macs * quarter,
        where, tokens, inv_rms, home[2], home[3], *early,
    )
    return (keys, grad_tokens, weight_step, gain_step[0])


def solution(mesh):
    fine = Mesh(mesh.devices.reshape(SIZES), AXES)
    matrix, vector = P(AXES, None), P(AXES)
    return jax.shard_map(
        body,
        mesh=fine,
        in_specs=(matrix, vector, matrix, matrix, matrix, matrix, vector, vector),
        out_specs=(matrix, matrix, matrix, vector),
        check_vma=False,
    )
```

```python
import functools

import jax
import jax.numpy as jnp
import numpy as np
from jax import lax
from jax.experimental import pallas as pl
from jax.experimental.pallas import tpu as pltpu
from jax.sharding import Mesh, PartitionSpec as P

RUN = 128
AXES = ("y", "xh", "core", "z", "xl")
SIZES = (4, 2, 2, 8, 2)

eps_norm = 1e-06
beta_one = 0.9
beta_two = 0.999
eps_adam = 1e-08

bf16 = jnp.bfloat16
f32 = jnp.float32


def index_of(y, x, z, c):
    return (((y * 2 + x // 2) * 2 + c) * 8 + z) * 2 + x % 2


def move(value, target):
    pairs = []
    for y in range(4):
        for x in range(4):
            for z in range(8):
                for c in range(2):
                    ty, tx, tz, tc = target(y, x, z, c)
                    pairs.append((index_of(y, x, z, c), index_of(ty % 4, tx % 4, tz % 8, tc % 2)))
    return lax.ppermute(value, AXES, pairs)


def along_y(value, step):
    return move(value, lambda y, x, z, c: (y + step, x, z, c))


def along_x(value, flip):
    return move(value, lambda y, x, z, c: (y, x ^ flip, z, c))


def swap(value):
    return move(value, lambda y, x, z, c: (y, x, z, 1 - c))


STEPS = (1, -1, 2)


def dot(a, b, ca, cb):
    return lax.dot_general(a, b, (((ca,), (cb,)), ((), ())), preferred_element_type=f32)


def call(kernel, outs, scratch, flops, *operands):
    specs = [pl.BlockSpec(memory_space=pltpu.SMEM if v.dtype == jnp.int32 and v.ndim == 1 else pltpu.VMEM) for v in operands]
    moved = sum(v.size * v.dtype.itemsize for v in operands)
    return pl.pallas_call(
        kernel,
        out_shape=[jax.ShapeDtypeStruct(shape, dtype) for shape, dtype in outs],
        in_specs=specs,
        out_specs=[pl.BlockSpec(memory_space=pltpu.VMEM)] * len(outs),
        scratch_shapes=[pltpu.VMEM(shape, dtype) for shape, dtype in scratch],
        compiler_params=pltpu.CompilerParams(vmem_limit_bytes=16 * 2**20),
        cost_estimate=pl.CostEstimate(flops=flops, bytes_accessed=moved, transcendentals=0),
    )(*operands)


def exchange_z(blocks):
    return lax.all_to_all(blocks, "z", split_axis=0, concat_axis=0, tiled=True)


def adam_step(grad, first, second):
    first = beta_one * first + (1.0 - beta_one) * grad
    second = beta_two * second + (1.0 - beta_two) * grad * grad
    return first / (jnp.sqrt(second) + eps_adam)


def feature_table(quarter, rows):
    place = np.arange(quarter)
    r, z, k, other = place % rows, place // rows % 8, place // (8 * rows) % 4, place // (32 * rows)
    table = []
    for x in range(4):
        for c in range(2):
            at = x ^ k
            table.append((((at // 2) * 2 + (c ^ other)) * 8 + z) * 2 * rows + at % 2 * rows + r)
    return np.stack(table).astype(np.int32)


def one_hot(where, table):
    width = table.shape[1]
    place = table[pl.ds(where[1], 1), :]
    feature = lax.broadcasted_iota(jnp.int32, (width, width), 0)
    return jnp.where(feature == place, 1.0, 0.0).astype(bf16)


def column_of(row):
    n = row.shape[1]
    same = lax.broadcasted_iota(jnp.int32, (n, n), 0) == lax.broadcasted_iota(jnp.int32, (n, n), 1)
    return jnp.sum(jnp.where(same, jnp.broadcast_to(row, (n, n)), 0.0), axis=1, keepdims=True)


def row_of(column):
    n = column.shape[0]
    same = lax.broadcasted_iota(jnp.int32, (n, n), 0) == lax.broadcasted_iota(jnp.int32, (n, n), 1)
    return jnp.sum(jnp.where(same, jnp.broadcast_to(column, (n, n)), 0.0), axis=0, keepdims=True)


def quantize_kernel(master, gain, shard, weight):
    one_gain = 1.0 + column_of(gain[...])
    for n in range(master.shape[1] // RUN):
        at = slice(n * RUN, (n + 1) * RUN)
        run = master[:, at]
        scale = (jnp.max(jnp.abs(run), axis=1, keepdims=True) + 1e-06) / 127.0
        value = jnp.floor(run / scale + 0.5) * scale
        weight[:, at] = value
        value = (value * one_gain).astype(bf16)
        for m in range(shard.shape[0]):
            shard[m, :, at] = value


def place(where, step, width):
    return pl.multiple_of(lax.rem(where[0] + step + 4, 4) * width, 128)


def norm_kernel(where, table, tokens, own, two, up, down, inv_rms, rounded, chosen):
    choice = one_hot(where, table)
    width = choice.shape[0]
    values = tokens[...].astype(f32)
    inv = lax.rsqrt(jnp.mean(values * values, axis=1, keepdims=True) + eps_norm)
    inv_rms[...] = inv
    tok = values.shape[0]
    for n in range(4):
        part = tokens[:, n * width : (n + 1) * width].astype(f32) * inv
        rounded[n * tok : (n + 1) * tok] = part.astype(bf16)
    chosen[...] = dot(rounded[...], choice, 1, 0).astype(bf16)
    for s, out in zip(STEPS + (0,), (two, up, down, own)):
        out[...] = chosen[pl.ds(place(where, s, tok), tok)]


def home_kernel(*refs):
    chunks, fs, cs, outs, ws = refs[:8], refs[8], refs[9], refs[10:14], refs[14]
    rows, width = chunks[0].shape[0], ws.shape[0]
    tok = outs[0].shape[0]
    for n in range(8):
        ws[n * rows : (n + 1) * rows] = chunks[n][...]
    step = 2 * RUN
    for at in range(0, width, step):
        to = min(at + step, width)
        part = dot(cs[...], ws[at:to], 1, 1).astype(bf16)
        for j in range(4):
            outs[j][:, at:to] = part[j * tok : (j + 1) * tok]
    for at in range(0, ws.shape[1], step):
        part = dot(fs[...], ws[:, at : at + step], 1, 0).astype(bf16)
        for j in range(4):
            outs[j][:, width + at : width + at + step] = part[j * tok : (j + 1) * tok]


def term_kernel(*refs):
    feats, cots, outs, theirs, fs, cs = refs[:4], refs[4:8], refs[8:12], refs[12], refs[13], refs[14]
    tok = feats[0].shape[0]
    for j in range(4):
        cs[j * tok : (j + 1) * tok] = cots[j][...]
        fs[j * tok : (j + 1) * tok] = feats[j][...]
    rows, half = outs[0].shape[0], theirs.shape[0]
    step = 2 * RUN
    for at in range(0, cs.shape[1], step):
        part = dot(fs[...], cs[:, at : at + step], 0, 0)
        theirs[:, at : at + step] = part[half:].astype(bf16)
        for k in range(4):
            outs[k][:, at : at + step] = part[k * rows : (k + 1) * rows]


def add_kernel(one, two, three, theirs, *outs):
    rows = one.shape[0]
    for k, (ref, out) in enumerate(zip((one, two, three), outs)):
        out[...] = (ref[...] + theirs[(k + 1) * rows : (k + 2) * rows].astype(f32)).astype(bf16)


def chunk_kernel(mine, theirs, one, two, three, out, total):
    rows = out.shape[1]
    total[...] = mine[...] + theirs[: mine.shape[0]].astype(f32) + one[...].astype(f32) + two[...].astype(f32) + three[...].astype(f32)
    for n in range(out.shape[0]):
        out[n] = total[n * rows : (n + 1) * rows].astype(bf16)


def early_kernel(where, table, tokens, own, two, scaled, inner, keys, choice):
    choice[...] = one_hot(where, table)
    width, tok = choice.shape[0], inner.shape[0]
    both = dot(jnp.concatenate([own[:, :width], two[:, :width]]), choice[...], 1, 1)
    total = jnp.zeros(inner.shape, f32)
    for n, s in enumerate((0, STEPS[0])):
        part = both[n * tok : (n + 1) * tok]
        scaled[:, n * width : (n + 1) * width] = part
        total += jnp.sum(part * tokens[:, pl.ds(place(where, s, width), width)].astype(f32), axis=1, keepdims=True)
    inner[...] = total
    keys[...] = own[:, width:].astype(f32) + two[:, width:].astype(f32)


def last_kernel(where, tokens, inv_rms, up, down, early, early_inner, early_keys, choice, keys, grad):
    width, tok = choice.shape[0], inv_rms.shape[0]
    keys[...] = (early_keys[...] + up[:, width:].astype(f32) + down[:, width:].astype(f32)).astype(bf16)
    inv = inv_rms[...]
    inner = early_inner[...]
    both = dot(jnp.concatenate([up[:, :width], down[:, :width]]), choice[...], 1, 1)
    parts = []
    for n, s in enumerate(STEPS[1:]):
        part = both[n * tok : (n + 1) * tok]
        parts.append(part)
        inner += jnp.sum(part * tokens[:, pl.ds(place(where, s, width), width)].astype(f32), axis=1, keepdims=True)
    inner = inner * inv * (1.0 / tokens.shape[1])
    for n, s in enumerate(STEPS[1:] + (0, STEPS[0])):
        at = pl.ds(place(where, s, width), width)
        normed = tokens[:, at].astype(f32) * inv
        part = parts[n] if n < 2 else early[:, (n - 2) * width : (n - 1) * width]
        grad[:, at] = (inv * (part - normed * inner)).astype(bf16)


def step_kernel(count, summed, weight, gain, w_first, w_second, g_first, g_second, w_step, g_step):
    grad = summed[0].astype(f32)
    for n in range(1, summed.shape[0]):
        grad = grad + summed[n].astype(f32)
    one_gain = 1.0 + column_of(gain[...])
    w_step[...] = adam_step(grad * one_gain / count, w_first[...], w_second[...])
    gain_grad = row_of(jnp.sum(weight[...] * grad, axis=1, keepdims=True)) / count
    g_step[...] = adam_step(gain_grad, g_first[...], g_second[...])


def body(tokens, gain_master, weight_master, cotangent, w_first, w_second, gain_first, gain_second):
    y, xh, c, z, xl = [lax.axis_index(name) for name in AXES]
    tok_count, model_width = tokens.shape
    shard_rows, key_width = weight_master.shape
    total = tok_count * 256
    quarter = model_width // 4
    eighth = quarter // 2
    chunk = eighth // 4
    macs = tok_count * quarter * 4
    where = jnp.stack([y, 4 * xh + 2 * xl + c]).astype(jnp.int32)
    table = jnp.asarray(feature_table(quarter, shard_rows))

    gain_row = gain_master[None]
    shard, weight = call(
        quantize_kernel,
        [((8, shard_rows, key_width), bf16), ((shard_rows, key_width), f32)],
        [],
        100000,
        weight_master, gain_row,
    )
    column = exchange_z(shard).reshape(chunk, key_width)

    own, *sends, inv_rms = call(
        norm_kernel,
        [((tok_count, quarter), bf16)] * 4 + [((tok_count, 1), f32)],
        [((4 * tok_count, quarter), bf16)] * 2,
        2 * macs * quarter,
        where, table, tokens,
    )
    shard, cot_sent = lax.optimization_barrier((shard, cotangent))
    cots = [cotangent] + [along_y(cot_sent, s) for s in STEPS]
    column, cots = lax.optimization_barrier((column, cots))
    feats = [own] + [along_y(v, s) for v, s in zip(sends, STEPS)]
    mine = [column] + [along_x(column, k) for k in (1, 2, 3)]

    feats, mine = lax.optimization_barrier((feats, mine))
    gathered = mine + [swap(v) for v in mine]
    *term, theirs, all_feats, all_cots = call(
        term_kernel,
        [((chunk, key_width), f32)] * 4
        + [((eighth, key_width), bf16), ((4 * tok_count, quarter), bf16), ((4 * tok_count, key_width), bf16)],
        [],
        2 * macs * key_width,
        *feats, *cots,
    )
    theirs = swap(theirs)
    moved = call(add_kernel, [((chunk, key_width), bf16)] * 3, [], 100000, *term[1:], theirs)
    moved = [along_x(v, k) for k, v in zip((1, 2, 3), moved)]
    (summed,) = call(
        chunk_kernel,
        [((8, shard_rows, key_width), bf16)],
        [((chunk, key_width), f32)],
        100000,
        term[0], theirs, *moved,
    )
    summed = exchange_z(summed)
    weight_step, gain_step = call(
        functools.partial(step_kernel, total),
        [((shard_rows, key_width), f32), ((1, shard_rows), f32)],
        [],
        100000,
        summed, weight, gain_row, w_first, w_second, gain_first[None], gain_second[None],
    )

    parts = call(
        home_kernel,
        [((tok_count, quarter + key_width), bf16)] * 4,
        [((quarter, key_width), bf16)],
        4 * macs * key_width,
        *gathered, all_feats, all_cots,
    )
    home = [parts[0]] + [along_y(v, -s) for v, s in zip(parts[1:], STEPS)]

    half = (tok_count, 2 * quarter)
    early = call(
        early_kernel,
        [(half, f32), ((tok_count, 1), f32), ((tok_count, key_width), f32), ((quarter, quarter), bf16)],
        [],
        macs * quarter,
        where, table, tokens, home[0], home[1],
    )
    keys, grad_tokens = call(
        last_kernel,
        [((tok_count, key_width), bf16), ((tok_count, model_width), bf16)],
        [],
        macs * quarter,
        where, tokens, inv_rms, home[2], home[3], *early,
    )
    return (keys, grad_tokens, weight_step, gain_step[0])


def solution(mesh):
    fine = Mesh(mesh.devices.reshape(SIZES), AXES)
    matrix, vector = P(AXES, None), P(AXES)
    return jax.shard_map(
        body,
        mesh=fine,
        in_specs=(matrix, vector, matrix, matrix, matrix, matrix, vector, vector),
        out_specs=(matrix, matrix, matrix, vector),
        check_vma=False,
    )
```

```python
import functools

import jax
import jax.numpy as jnp
import numpy as np
from jax import lax
from jax.experimental import pallas as pl
from jax.experimental.pallas import tpu as pltpu
from jax.sharding import Mesh, PartitionSpec as P

RUN = 128
AXES = ("y", "xh", "core", "z", "xl")
SIZES = (4, 2, 2, 8, 2)

eps_norm = 1e-06
beta_one = 0.9
beta_two = 0.999
eps_adam = 1e-08

bf16 = jnp.bfloat16
f32 = jnp.float32


def index_of(y, x, z, c):
    return (((y * 2 + x // 2) * 2 + c) * 8 + z) * 2 + x % 2


def move(value, target):
    pairs = []
    for y in range(4):
        for x in range(4):
            for z in range(8):
                for c in range(2):
                    ty, tx, tz, tc = target(y, x, z, c)
                    pairs.append((index_of(y, x, z, c), index_of(ty % 4, tx % 4, tz % 8, tc % 2)))
    return lax.ppermute(value, AXES, pairs)


def along_y(value, step):
    return move(value, lambda y, x, z, c: (y + step, x, z, c))


def along_x(value, flip):
    return move(value, lambda y, x, z, c: (y, x ^ flip, z, c))


def around_x(value):
    return move(value, lambda y, x, z, c: (y, x ^ (1 + 2 * c), z, c))


def swap(value):
    return move(value, lambda y, x, z, c: (y, x, z, 1 - c))


STEPS = (1, -1, 2)


def dot(a, b, ca, cb):
    return lax.dot_general(a, b, (((ca,), (cb,)), ((), ())), preferred_element_type=f32)


def call(kernel, outs, scratch, flops, *operands):
    specs = [pl.BlockSpec(memory_space=pltpu.SMEM if v.dtype == jnp.int32 and v.ndim == 1 else pltpu.VMEM) for v in operands]
    moved = sum(v.size * v.dtype.itemsize for v in operands)
    return pl.pallas_call(
        kernel,
        out_shape=[jax.ShapeDtypeStruct(shape, dtype) for shape, dtype in outs],
        in_specs=specs,
        out_specs=[pl.BlockSpec(memory_space=pltpu.VMEM)] * len(outs),
        scratch_shapes=[pltpu.VMEM(shape, dtype) for shape, dtype in scratch],
        compiler_params=pltpu.CompilerParams(vmem_limit_bytes=16 * 2**20),
        cost_estimate=pl.CostEstimate(flops=flops, bytes_accessed=moved, transcendentals=0),
    )(*operands)


def exchange_z(blocks):
    return lax.all_to_all(blocks, "z", split_axis=0, concat_axis=0, tiled=True)


def adam_step(grad, first, second):
    first = beta_one * first + (1.0 - beta_one) * grad
    second = beta_two * second + (1.0 - beta_two) * grad * grad
    return first / (jnp.sqrt(second) + eps_adam)


def feature_table(quarter, rows):
    place = np.arange(quarter)
    r, z, k, other = place % rows, place // rows % 8, place // (8 * rows) % 4, place // (32 * rows)
    table = []
    for x in range(4):
        for c in range(2):
            at = x ^ k
            table.append((((at // 2) * 2 + (c ^ other)) * 8 + z) * 2 * rows + at % 2 * rows + r)
    return np.stack(table).astype(np.int32)


def one_hot(where, table):
    width = table.shape[1]
    place = table[pl.ds(where[1], 1), :]
    feature = lax.broadcasted_iota(jnp.int32, (width, width), 0)
    return jnp.where(feature == place, 1.0, 0.0).astype(bf16)


def column_of(row):
    n = row.shape[1]
    same = lax.broadcasted_iota(jnp.int32, (n, n), 0) == lax.broadcasted_iota(jnp.int32, (n, n), 1)
    return jnp.sum(jnp.where(same, jnp.broadcast_to(row, (n, n)), 0.0), axis=1, keepdims=True)


def row_of(column):
    n = column.shape[0]
    same = lax.broadcasted_iota(jnp.int32, (n, n), 0) == lax.broadcasted_iota(jnp.int32, (n, n), 1)
    return jnp.sum(jnp.where(same, jnp.broadcast_to(column, (n, n)), 0.0), axis=0, keepdims=True)


def quantize_kernel(master, gain, shard, weight):
    one_gain = 1.0 + column_of(gain[...])
    for n in range(master.shape[1] // RUN):
        at = slice(n * RUN, (n + 1) * RUN)
        run = master[:, at]
        scale = (jnp.max(jnp.abs(run), axis=1, keepdims=True) + 1e-06) / 127.0
        value = jnp.floor(run / scale + 0.5) * scale
        weight[:, at] = value
        value = (value * one_gain).astype(bf16)
        for m in range(shard.shape[0]):
            shard[m, :, at] = value


def place(where, step, width):
    return pl.multiple_of(lax.rem(where[0] + step + 4, 4) * width, 128)


def norm_kernel(where, table, tokens, own, two, up, down, inv_rms, rounded, chosen):
    choice = one_hot(where, table)
    width = choice.shape[0]
    values = tokens[...].astype(f32)
    inv = lax.rsqrt(jnp.mean(values * values, axis=1, keepdims=True) + eps_norm)
    inv_rms[...] = inv
    tok = values.shape[0]
    for n in range(4):
        part = tokens[:, n * width : (n + 1) * width].astype(f32) * inv
        rounded[n * tok : (n + 1) * tok] = part.astype(bf16)
    chosen[...] = dot(rounded[...], choice, 1, 0).astype(bf16)
    for s, out in zip(STEPS + (0,), (two, up, down, own)):
        out[...] = chosen[pl.ds(place(where, s, tok), tok)]


def home_kernel(*refs):
    chunks, fs, cs, outs, ws = refs[:8], refs[8], refs[9], refs[10:14], refs[14]
    rows, width = chunks[0].shape[0], ws.shape[0]
    tok = outs[0].shape[0]
    for n in range(8):
        ws[n * rows : (n + 1) * rows] = chunks[n][...]
    step = 2 * RUN
    for at in range(0, width, step):
        to = min(at + step, width)
        part = dot(cs[...], ws[at:to], 1, 1).astype(bf16)
        for j in range(4):
            outs[j][:, at:to] = part[j * tok : (j + 1) * tok]
    for at in range(0, ws.shape[1], step):
        part = dot(fs[...], ws[:, at : at + step], 1, 0).astype(bf16)
        for j in range(4):
            outs[j][:, width + at : width + at + step] = part[j * tok : (j + 1) * tok]


def term_kernel(*refs):
    feats, cots, outs, theirs, fs, cs = refs[:4], refs[4:8], refs[8:12], refs[12], refs[13], refs[14]
    tok = feats[0].shape[0]
    for j in range(4):
        cs[j * tok : (j + 1) * tok] = cots[j][...]
        fs[j * tok : (j + 1) * tok] = feats[j][...]
    rows, half = outs[0].shape[0], theirs.shape[0]
    step = 2 * RUN
    for at in range(0, cs.shape[1], step):
        part = dot(fs[...], cs[:, at : at + step], 0, 0)
        theirs[:, at : at + step] = part[half:].astype(bf16)
        for k in range(4):
            outs[k][:, at : at + step] = part[k * rows : (k + 1) * rows]


def far_kernel(two, theirs, out):
    rows = two.shape[0]
    out[...] = (two[...] + theirs[2 * rows : 3 * rows].astype(f32)).astype(bf16)


def near_kernel(where, one, three, theirs, passed, to_one, to_three):
    rows, core = one.shape[0], lax.rem(where[1], 2)
    extra = passed[...].astype(f32)
    to_one[...] = (one[...] + theirs[rows : 2 * rows].astype(f32) + jnp.where(core == 1, extra, 0.0)).astype(bf16)
    to_three[...] = (three[...] + theirs[3 * rows :].astype(f32) + jnp.where(core == 0, extra, 0.0)).astype(bf16)


def chunk_kernel(mine, theirs, one, three, out, total):
    rows = out.shape[1]
    total[...] = mine[...] + theirs[: mine.shape[0]].astype(f32) + one[...].astype(f32) + three[...].astype(f32)
    for n in range(out.shape[0]):
        out[n] = total[n * rows : (n + 1) * rows].astype(bf16)


def early_kernel(where, table, tokens, own, two, scaled, inner, keys, choice):
    choice[...] = one_hot(where, table)
    width, tok = choice.shape[0], inner.shape[0]
    both = dot(jnp.concatenate([own[:, :width], two[:, :width]]), choice[...], 1, 1)
    total = jnp.zeros(inner.shape, f32)
    for n, s in enumerate((0, STEPS[0])):
        part = both[n * tok : (n + 1) * tok]
        scaled[:, n * width : (n + 1) * width] = part
        total += jnp.sum(part * tokens[:, pl.ds(place(where, s, width), width)].astype(f32), axis=1, keepdims=True)
    inner[...] = total
    keys[...] = own[:, width:].astype(f32) + two[:, width:].astype(f32)


def last_kernel(where, tokens, inv_rms, up, down, early, early_inner, early_keys, choice, keys, grad):
    width, tok = choice.shape[0], inv_rms.shape[0]
    keys[...] = (early_keys[...] + up[:, width:].astype(f32) + down[:, width:].astype(f32)).astype(bf16)
    inv = inv_rms[...]
    inner = early_inner[...]
    both = dot(jnp.concatenate([up[:, :width], down[:, :width]]), choice[...], 1, 1)
    parts = []
    for n, s in enumerate(STEPS[1:]):
        part = both[n * tok : (n + 1) * tok]
        parts.append(part)
        inner += jnp.sum(part * tokens[:, pl.ds(place(where, s, width), width)].astype(f32), axis=1, keepdims=True)
    inner = inner * inv * (1.0 / tokens.shape[1])
    for n, s in enumerate(STEPS[1:] + (0, STEPS[0])):
        at = pl.ds(place(where, s, width), width)
        normed = tokens[:, at].astype(f32) * inv
        part = parts[n] if n < 2 else early[:, (n - 2) * width : (n - 1) * width]
        grad[:, at] = (inv * (part - normed * inner)).astype(bf16)


def step_kernel(count, summed, weight, gain, w_first, w_second, g_first, g_second, w_step, g_step):
    grad = summed[0].astype(f32)
    for n in range(1, summed.shape[0]):
        grad = grad + summed[n].astype(f32)
    one_gain = 1.0 + column_of(gain[...])
    w_step[...] = adam_step(grad * one_gain / count, w_first[...], w_second[...])
    gain_grad = row_of(jnp.sum(weight[...] * grad, axis=1, keepdims=True)) / count
    g_step[...] = adam_step(gain_grad, g_first[...], g_second[...])


def body(tokens, gain_master, weight_master, cotangent, w_first, w_second, gain_first, gain_second):
    y, xh, c, z, xl = [lax.axis_index(name) for name in AXES]
    tok_count, model_width = tokens.shape
    shard_rows, key_width = weight_master.shape
    total = tok_count * 256
    quarter = model_width // 4
    eighth = quarter // 2
    chunk = eighth // 4
    macs = tok_count * quarter * 4
    where = jnp.stack([y, 4 * xh + 2 * xl + c]).astype(jnp.int32)
    table = jnp.asarray(feature_table(quarter, shard_rows))

    gain_row = gain_master[None]
    shard, weight = call(
        quantize_kernel,
        [((8, shard_rows, key_width), bf16), ((shard_rows, key_width), f32)],
        [],
        100000,
        weight_master, gain_row,
    )
    column = exchange_z(shard).reshape(chunk, key_width)

    own, *sends, inv_rms = call(
        norm_kernel,
        [((tok_count, quarter), bf16)] * 4 + [((tok_count, 1), f32)],
        [((4 * tok_count, quarter), bf16)] * 2,
        2 * macs * quarter,
        where, table, tokens,
    )
    shard, cot_sent = lax.optimization_barrier((shard, cotangent))
    cots = [cotangent] + [along_y(cot_sent, s) for s in STEPS]
    column, cots = lax.optimization_barrier((column, cots))
    feats = [own] + [along_y(v, s) for v, s in zip(sends, STEPS)]
    mine = [column] + [along_x(column, k) for k in (1, 2, 3)]

    feats, mine = lax.optimization_barrier((feats, mine))
    gathered = mine + [swap(v) for v in mine]
    *term, theirs, all_feats, all_cots = call(
        term_kernel,
        [((chunk, key_width), f32)] * 4
        + [((eighth, key_width), bf16), ((4 * tok_count, quarter), bf16), ((4 * tok_count, key_width), bf16)],
        [],
        2 * macs * key_width,
        *feats, *cots,
    )
    theirs = swap(theirs)
    (far,) = call(far_kernel, [((chunk, key_width), bf16)], [], 100000, term[2], theirs)
    passed = around_x(far)
    parts = call(
        home_kernel,
        [((tok_count, quarter + key_width), bf16)] * 4,
        [((quarter, key_width), bf16)],
        4 * macs * key_width,
        *gathered, all_feats, all_cots,
    )
    theirs, parts = lax.optimization_barrier((theirs, parts))
    to_one, to_three = call(
        near_kernel, [((chunk, key_width), bf16)] * 2, [], 100000, where, term[1], term[3], theirs, passed
    )
    to_one, last_part = lax.optimization_barrier((to_one, parts[3]))
    parts = [*parts[:3], last_part]
    moved = [along_x(to_one, 1), along_x(to_three, 3)]
    home = [parts[0]] + [along_y(v, -s) for v, s in zip(parts[1:], STEPS)]

    (summed,) = call(
        chunk_kernel,
        [((8, shard_rows, key_width), bf16)],
        [((chunk, key_width), f32)],
        100000,
        term[0], theirs, *moved,
    )
    summed = exchange_z(summed)
    weight_step, gain_step = call(
        functools.partial(step_kernel, total),
        [((shard_rows, key_width), f32), ((1, shard_rows), f32)],
        [],
        100000,
        summed, weight, gain_row, w_first, w_second, gain_first[None], gain_second[None],
    )

    half = (tok_count, 2 * quarter)
    early = call(
        early_kernel,
        [(half, f32), ((tok_count, 1), f32), ((tok_count, key_width), f32), ((quarter, quarter), bf16)],
        [],
        macs * quarter,
        where, table, tokens, home[0], home[1],
    )
    keys, grad_tokens = call(
        last_kernel,
        [((tok_count, key_width), bf16), ((tok_count, model_width), bf16)],
        [],
        50 * macs * quarter,
        where, tokens, inv_rms, home[2], home[3], *early,
    )
    return (keys, grad_tokens, weight_step, gain_step[0])


def solution(mesh):
    fine = Mesh(mesh.devices.reshape(SIZES), AXES)
    matrix, vector = P(AXES, None), P(AXES)
    return jax.shard_map(
        body,
        mesh=fine,
        in_specs=(matrix, vector, matrix, matrix, matrix, matrix, vector, vector),
        out_specs=(matrix, matrix, matrix, vector),
        check_vma=False,
    )
```

```python
import functools

import jax
import jax.numpy as jnp
import numpy as np
from jax import lax
from jax.experimental import pallas as pl
from jax.experimental.pallas import tpu as pltpu
from jax.sharding import Mesh, PartitionSpec as P

RUN = 128
AXES = ("y", "xh", "core", "z", "xl")
SIZES = (4, 2, 2, 8, 2)

eps_norm = 1e-06
beta_one = 0.9
beta_two = 0.999
eps_adam = 1e-08

bf16 = jnp.bfloat16
f32 = jnp.float32


def index_of(y, x, z, c):
    return (((y * 2 + x // 2) * 2 + c) * 8 + z) * 2 + x % 2


def move(value, target):
    pairs = []
    for y in range(4):
        for x in range(4):
            for z in range(8):
                for c in range(2):
                    ty, tx, tz, tc = target(y, x, z, c)
                    pairs.append((index_of(y, x, z, c), index_of(ty % 4, tx % 4, tz % 8, tc % 2)))
    return lax.ppermute(value, AXES, pairs)


def along_y(value, step):
    return move(value, lambda y, x, z, c: (y + step, x, z, c))


def along_x(value, flip):
    return move(value, lambda y, x, z, c: (y, x ^ flip, z, c))


def around_x(value):
    return move(value, lambda y, x, z, c: (y, x ^ (1 + 2 * c), z, c))


def swap(value):
    return move(value, lambda y, x, z, c: (y, x, z, 1 - c))


STEPS = (1, -1, 2)


def dot(a, b, ca, cb):
    return lax.dot_general(a, b, (((ca,), (cb,)), ((), ())), preferred_element_type=f32)


def call(kernel, outs, scratch, flops, *operands):
    specs = [pl.BlockSpec(memory_space=pltpu.SMEM if v.dtype == jnp.int32 and v.ndim == 1 else pltpu.VMEM) for v in operands]
    moved = sum(v.size * v.dtype.itemsize for v in operands)
    return pl.pallas_call(
        kernel,
        out_shape=[jax.ShapeDtypeStruct(shape, dtype) for shape, dtype in outs],
        in_specs=specs,
        out_specs=[pl.BlockSpec(memory_space=pltpu.VMEM)] * len(outs),
        scratch_shapes=[pltpu.VMEM(shape, dtype) for shape, dtype in scratch],
        compiler_params=pltpu.CompilerParams(vmem_limit_bytes=16 * 2**20),
        cost_estimate=pl.CostEstimate(flops=flops, bytes_accessed=moved, transcendentals=0),
    )(*operands)


def exchange_z(blocks):
    return lax.all_to_all(blocks, "z", split_axis=0, concat_axis=0, tiled=True)


def adam_step(grad, first, second):
    first = beta_one * first + (1.0 - beta_one) * grad
    second = beta_two * second + (1.0 - beta_two) * grad * grad
    return first / (jnp.sqrt(second) + eps_adam)


def feature_table(quarter, rows):
    place = np.arange(quarter)
    r, z, k, other = place % rows, place // rows % 8, place // (8 * rows) % 4, place // (32 * rows)
    table = []
    for x in range(4):
        for c in range(2):
            at = x ^ k
            table.append((((at // 2) * 2 + (c ^ other)) * 8 + z) * 2 * rows + at % 2 * rows + r)
    return np.stack(table).astype(np.int32)


def one_hot(where, table):
    width = table.shape[1]
    place = table[pl.ds(where[1], 1), :]
    feature = lax.broadcasted_iota(jnp.int32, (width, width), 0)
    return jnp.where(feature == place, 1.0, 0.0).astype(bf16)


def column_of(row):
    n = row.shape[1]
    same = lax.broadcasted_iota(jnp.int32, (n, n), 0) == lax.broadcasted_iota(jnp.int32, (n, n), 1)
    return jnp.sum(jnp.where(same, jnp.broadcast_to(row, (n, n)), 0.0), axis=1, keepdims=True)


def row_of(column):
    n = column.shape[0]
    same = lax.broadcasted_iota(jnp.int32, (n, n), 0) == lax.broadcasted_iota(jnp.int32, (n, n), 1)
    return jnp.sum(jnp.where(same, jnp.broadcast_to(column, (n, n)), 0.0), axis=0, keepdims=True)


def quantize_kernel(master, gain, shard, weight):
    one_gain = 1.0 + column_of(gain[...])
    for n in range(master.shape[1] // RUN):
        at = slice(n * RUN, (n + 1) * RUN)
        run = master[:, at]
        scale = (jnp.max(jnp.abs(run), axis=1, keepdims=True) + 1e-06) / 127.0
        value = jnp.floor(run / scale + 0.5) * scale
        weight[:, at] = value
        value = (value * one_gain).astype(bf16)
        for m in range(shard.shape[0]):
            shard[m, :, at] = value


def place(where, step, width):
    return pl.multiple_of(lax.rem(where[0] + step + 4, 4) * width, 128)


def norm_kernel(where, table, tokens, own, two, up, down, inv_rms, rounded, chosen):
    choice = one_hot(where, table)
    width = choice.shape[0]
    values = tokens[...].astype(f32)
    inv = lax.rsqrt(jnp.mean(values * values, axis=1, keepdims=True) + eps_norm)
    inv_rms[...] = inv
    tok = values.shape[0]
    for n in range(4):
        part = tokens[:, n * width : (n + 1) * width].astype(f32) * inv
        rounded[n * tok : (n + 1) * tok] = part.astype(bf16)
    chosen[...] = dot(rounded[...], choice, 1, 0).astype(bf16)
    for s, out in zip(STEPS + (0,), (two, up, down, own)):
        out[...] = chosen[pl.ds(place(where, s, tok), tok)]


def home_kernel(*refs):
    chunks, fs, cs, outs, ws = refs[:8], refs[8], refs[9], refs[10:14], refs[14]
    rows, width = chunks[0].shape[0], ws.shape[0]
    tok = outs[0].shape[0]
    for n in range(8):
        ws[n * rows : (n + 1) * rows] = chunks[n][...]
    step = 2 * RUN
    for at in range(0, width, step):
        to = min(at + step, width)
        part = dot(cs[...], ws[at:to], 1, 1).astype(bf16)
        for j in range(4):
            outs[j][:, at:to] = part[j * tok : (j + 1) * tok]
    for at in range(0, ws.shape[1], step):
        part = dot(fs[...], ws[:, at : at + step], 1, 0).astype(bf16)
        for j in range(4):
            outs[j][:, width + at : width + at + step] = part[j * tok : (j + 1) * tok]


def theirs_kernel(*refs):
    feats, cots, theirs, fs, cs = refs[:4], refs[4:8], refs[8], refs[9], refs[10]
    tok, half = feats[0].shape[0], theirs.shape[0]
    for j in range(4):
        cs[j * tok : (j + 1) * tok] = cots[j][...]
        fs[j * tok : (j + 1) * tok] = feats[j][...]
    step = 2 * RUN
    for at in range(0, cs.shape[1], step):
        theirs[:, at : at + step] = dot(fs[:, half:], cs[:, at : at + step], 0, 0).astype(bf16)


def term_kernel(fs, cs, *outs):
    rows = outs[0].shape[0]
    step = 2 * RUN
    for at in range(0, cs.shape[1], step):
        part = dot(fs[:, : 4 * rows], cs[:, at : at + step], 0, 0)
        for k in range(4):
            outs[k][:, at : at + step] = part[k * rows : (k + 1) * rows]


def far_kernel(two, theirs, out):
    rows = two.shape[0]
    out[...] = (two[...] + theirs[2 * rows : 3 * rows].astype(f32)).astype(bf16)


def near_kernel(where, one, three, theirs, passed, to_one, to_three):
    rows, core = one.shape[0], lax.rem(where[1], 2)
    extra = passed[...].astype(f32)
    to_one[...] = (one[...] + theirs[rows : 2 * rows].astype(f32) + jnp.where(core == 1, extra, 0.0)).astype(bf16)
    to_three[...] = (three[...] + theirs[3 * rows :].astype(f32) + jnp.where(core == 0, extra, 0.0)).astype(bf16)


def chunk_kernel(mine, theirs, one, three, out, total):
    rows = out.shape[1]
    total[...] = mine[...] + theirs[: mine.shape[0]].astype(f32) + one[...].astype(f32) + three[...].astype(f32)
    for n in range(out.shape[0]):
        out[n] = total[n * rows : (n + 1) * rows].astype(bf16)


def early_kernel(where, table, tokens, own, two, scaled, inner, keys, choice):
    choice[...] = one_hot(where, table)
    width, tok = choice.shape[0], inner.shape[0]
    both = dot(jnp.concatenate([own[:, :width], two[:, :width]]), choice[...], 1, 1)
    total = jnp.zeros(inner.shape, f32)
    for n, s in enumerate((0, STEPS[0])):
        part = both[n * tok : (n + 1) * tok]
        scaled[:, n * width : (n + 1) * width] = part
        total += jnp.sum(part * tokens[:, pl.ds(place(where, s, width), width)].astype(f32), axis=1, keepdims=True)
    inner[...] = total
    keys[...] = own[:, width:].astype(f32) + two[:, width:].astype(f32)


def last_kernel(where, tokens, inv_rms, up, down, early, early_inner, early_keys, choice, keys, grad):
    width, tok = choice.shape[0], inv_rms.shape[0]
    keys[...] = (early_keys[...] + up[:, width:].astype(f32) + down[:, width:].astype(f32)).astype(bf16)
    inv = inv_rms[...]
    inner = early_inner[...]
    both = dot(jnp.concatenate([up[:, :width], down[:, :width]]), choice[...], 1, 1)
    parts = []
    for n, s in enumerate(STEPS[1:]):
        part = both[n * tok : (n + 1) * tok]
        parts.append(part)
        inner += jnp.sum(part * tokens[:, pl.ds(place(where, s, width), width)].astype(f32), axis=1, keepdims=True)
    inner = inner * inv * (1.0 / tokens.shape[1])
    for n, s in enumerate(STEPS[1:] + (0, STEPS[0])):
        at = pl.ds(place(where, s, width), width)
        normed = tokens[:, at].astype(f32) * inv
        part = parts[n] if n < 2 else early[:, (n - 2) * width : (n - 1) * width]
        grad[:, at] = (inv * (part - normed * inner)).astype(bf16)


def step_kernel(count, summed, weight, gain, w_first, w_second, g_first, g_second, w_step, g_step):
    grad = summed[0].astype(f32)
    for n in range(1, summed.shape[0]):
        grad = grad + summed[n].astype(f32)
    one_gain = 1.0 + column_of(gain[...])
    w_step[...] = adam_step(grad * one_gain / count, w_first[...], w_second[...])
    gain_grad = row_of(jnp.sum(weight[...] * grad, axis=1, keepdims=True)) / count
    g_step[...] = adam_step(gain_grad, g_first[...], g_second[...])


def body(tokens, gain_master, weight_master, cotangent, w_first, w_second, gain_first, gain_second):
    y, xh, c, z, xl = [lax.axis_index(name) for name in AXES]
    tok_count, model_width = tokens.shape
    shard_rows, key_width = weight_master.shape
    total = tok_count * 256
    quarter = model_width // 4
    eighth = quarter // 2
    chunk = eighth // 4
    macs = tok_count * quarter * 4
    where = jnp.stack([y, 4 * xh + 2 * xl + c]).astype(jnp.int32)
    table = jnp.asarray(feature_table(quarter, shard_rows))

    gain_row = gain_master[None]
    shard, weight = call(
        quantize_kernel,
        [((8, shard_rows, key_width), bf16), ((shard_rows, key_width), f32)],
        [],
        100000,
        weight_master, gain_row,
    )
    column = exchange_z(shard).reshape(chunk, key_width)

    own, *sends, inv_rms = call(
        norm_kernel,
        [((tok_count, quarter), bf16)] * 4 + [((tok_count, 1), f32)],
        [((4 * tok_count, quarter), bf16)] * 2,
        2 * macs * quarter,
        where, table, tokens,
    )
    shard, cot_sent = lax.optimization_barrier((shard, cotangent))
    cots = [cotangent] + [along_y(cot_sent, s) for s in STEPS]
    column, cots = lax.optimization_barrier((column, cots))
    feats = [own] + [along_y(v, s) for v, s in zip(sends, STEPS)]
    mine = [column] + [along_x(column, k) for k in (1, 2, 3)]

    feats, mine = lax.optimization_barrier((feats, mine))
    gathered = mine + [swap(v) for v in mine]
    theirs, all_feats, all_cots = call(
        theirs_kernel,
        [((eighth, key_width), bf16), ((4 * tok_count, quarter), bf16), ((4 * tok_count, key_width), bf16)],
        [],
        macs * key_width,
        *feats, *cots,
    )
    term = call(term_kernel, [((chunk, key_width), f32)] * 4, [], macs * key_width, all_feats, all_cots)
    theirs = swap(theirs)
    (far,) = call(far_kernel, [((chunk, key_width), bf16)], [], 100000, term[2], theirs)
    passed = around_x(far)
    parts = call(
        home_kernel,
        [((tok_count, quarter + key_width), bf16)] * 4,
        [((quarter, key_width), bf16)],
        4 * macs * key_width,
        *gathered, all_feats, all_cots,
    )
    theirs, parts = lax.optimization_barrier((theirs, parts))
    to_one, to_three = call(
        near_kernel, [((chunk, key_width), bf16)] * 2, [], 100000, where, term[1], term[3], theirs, passed
    )
    to_one, last_part = lax.optimization_barrier((to_one, parts[3]))
    parts = [*parts[:3], last_part]
    moved = [along_x(to_one, 1), along_x(to_three, 3)]
    home = [parts[0]] + [along_y(v, -s) for v, s in zip(parts[1:], STEPS)]

    (summed,) = call(
        chunk_kernel,
        [((8, shard_rows, key_width), bf16)],
        [((chunk, key_width), f32)],
        100000,
        term[0], theirs, *moved,
    )
    summed = exchange_z(summed)
    weight_step, gain_step = call(
        functools.partial(step_kernel, total),
        [((shard_rows, key_width), f32), ((1, shard_rows), f32)],
        [],
        100000,
        summed, weight, gain_row, w_first, w_second, gain_first[None], gain_second[None],
    )

    half = (tok_count, 2 * quarter)
    early = call(
        early_kernel,
        [(half, f32), ((tok_count, 1), f32), ((tok_count, key_width), f32), ((quarter, quarter), bf16)],
        [],
        macs * quarter,
        where, table, tokens, home[0], home[1],
    )
    keys, grad_tokens = call(
        last_kernel,
        [((tok_count, key_width), bf16), ((tok_count, model_width), bf16)],
        [],
        50 * macs * quarter,
        where, tokens, inv_rms, home[2], home[3], *early,
    )
    return (keys, grad_tokens, weight_step, gain_step[0])


def solution(mesh):
    fine = Mesh(mesh.devices.reshape(SIZES), AXES)
    matrix, vector = P(AXES, None), P(AXES)
    return jax.shard_map(
        body,
        mesh=fine,
        in_specs=(matrix, vector, matrix, matrix, matrix, matrix, vector, vector),
        out_specs=(matrix, matrix, matrix, vector),
        check_vma=False,
    )
```
